256 devices in a mesh: group: 16 (over x, y), delay: 16 (over z, core).
Axes of the slice: x: 4, y: 4, z: 8, core: 2. Of those that a mesh axis runs over, the one named last changes fastest.
Arguments:
- retarded: bfloat16 [16, 256, 3, 256, 256], P('delay', 'group'), may hold values from -0.0234375 to 0.0234375
- block_row: int32 [16, 256, 3], P('delay', 'group'), may hold values from 0 to 3, as said below
- block_count: int32 [16, 256], P('delay', 'group'), may hold values from 1 to 3, as said below
- send_pick: int32 [16, 16, 16], P('delay'), may hold values from 0 to 3
- history: bfloat16 [16, 16384, 128], P('delay', 'group'), may hold values from -6 to 6
- incident: bfloat16 [4, 16384, 128], P(None, 'group'), may hold values from -6 to 6
- self_block: bfloat16 [16384, 1024], P('group'), may hold values from -0.1875 to 0.1875
- sheet_diag: float32 [16384], P('group'), may hold values from 1 to 1.6
Outputs:
- currents: bfloat16 [4, 16384, 128], P(None, 'group')
The draws below stay inside these ranges and needn't reach their ends.
Inputs may be any that keep to these rules, and one draw needn't show every extreme that they name: `block_row`: the live list places of one section, reading group and source group name distinct row blocks. `block_count`: list places at or beyond the count are ignored.
All inputs are finite; a program needn't handle non-finite values.
Results may differ from the reference program's by a relative error of at most 0.0085.
Values may be sent and summed in bfloat16 or wider, within the bound.
A program may use at most 128 MiB of HBM per device.

```python
import math
import jax
import jax.numpy as jnp
from jax import lax

BLK = 256
GBLK = 4
LPG = 3
EXC = 128
STEPS = 4
ITERS = 3
GROUPS = 16
DELAYS = 16
GROUP_ROWS = 1024
UNKNOWNS = 16384


def draw_block_row(key, part):
    key_list = jax.random.split(jax.random.fold_in(key, 11), DELAYS * GROUPS * GROUPS)
    row_list = jax.vmap(lambda subkey: jax.random.permutation(subkey, GBLK)[:LPG])(key_list)
    return row_list.reshape(DELAYS, GROUPS * GROUPS, LPG).astype(jnp.int32)


def draw_block_count(key, part):
    key_cap, key_load = jax.random.split(jax.random.fold_in(key, 23))
    ceiling = jax.random.randint(key_cap, (DELAYS, GROUPS, 1), 1, LPG + 1)
    counts = jnp.minimum(jax.random.randint(key_load, (DELAYS, GROUPS, GROUPS), 1, LPG + 1), ceiling)
    section = lax.broadcasted_iota(jnp.int32, (DELAYS, GROUPS, GROUPS), 0)
    reader = lax.broadcasted_iota(jnp.int32, (DELAYS, GROUPS, GROUPS), 1)
    source = lax.broadcasted_iota(jnp.int32, (DELAYS, GROUPS, GROUPS), 2)
    forced = source == (reader + section) % GROUPS
    counts = jnp.where(forced, LPG, counts)
    return counts.reshape(DELAYS, GROUPS * GROUPS).astype(jnp.int32)


def draw_send_pick(key, part):
    return jax.random.randint(jax.random.fold_in(key, 37), (DELAYS, GROUPS, GROUPS), 0, GBLK).astype(jnp.int32)


def level_of(stream_key, dims, shards, low, top_value):
    def one(dim, parts):
        heights = jax.random.uniform(jax.random.fold_in(jax.random.fold_in(stream_key, 6), dim), (parts,), jnp.float32, low / len(shards), top_value / len(shards))
        return jnp.repeat(jnp.exp(heights), dims[dim] // parts).reshape((-1,) + (1,) * (len(dims) - dim - 1))

    level = one(*shards[0])
    for cut in shards[1:]:
        level = level * one(*cut)
    return level


def bell_draw(key, extent, scale, most, shards=(), held_as=jnp.bfloat16):
    array = jax.random.normal(key, extent, jnp.float32) * scale
    if len(shards) > 0:
        array = level_of(key, extent, shards, -0.22, 0.18) * array
    return jnp.clip(array, min=-most, max=most).astype(held_as)


def setup_inputs(seed: int = 0) -> dict:
    arg_keys = jax.random.split(jax.random.key(seed), 9)
    return {
        "retarded": bell_draw(arg_keys[0], (DELAYS, GROUPS * GROUPS, LPG, BLK, BLK), (DELAYS * GROUPS * BLK) ** -0.5, 0.0234375, ((0, 16), (1, 16))),
        "block_row": draw_block_row(jax.random.fold_in(arg_keys[8], 71), 0),
        "block_count": draw_block_count(jax.random.fold_in(arg_keys[8], 71), 0),
        "send_pick": draw_send_pick(jax.random.fold_in(arg_keys[8], 71), 0),
        "history": bell_draw(arg_keys[4], (DELAYS, UNKNOWNS, EXC), 1.0, 6.0, ((0, 16), (1, 16))),
        "incident": bell_draw(arg_keys[5], (STEPS, UNKNOWNS, EXC), 1.0, 6.0, ((1, 16),)),
        "self_block": bell_draw(arg_keys[6], (UNKNOWNS, GROUP_ROWS), GROUP_ROWS ** -0.5, 0.1875, ((0, 16),)),
        "sheet_diag": jnp.clip(jnp.exp(math.log(1.6) - 0.47000364 * jax.random.uniform(arg_keys[7], (UNKNOWNS,), jnp.float32) ** level_of(arg_keys[7], (UNKNOWNS,), ((0, 16),), -0.2, 0.2)), 1.0, 1.6),
    }


def section_term(weights, row_list, live_count, picked, current):
    block_table = current.reshape(GROUPS * GBLK, BLK, EXC)
    block_index = (jnp.arange(GROUPS, dtype=jnp.int32) * GBLK + picked).astype(jnp.int32)
    blocks = block_table[block_index].astype(jnp.float32)
    terms = jnp.einsum("hlij,hjc->hlic", weights.astype(jnp.float32), blocks, precision=lax.Precision.HIGHEST)
    places = jnp.arange(LPG, dtype=jnp.int32)
    select = ((row_list[:, :, None] == jnp.arange(GBLK, dtype=jnp.int32)[None, None, :])
              & (places[None, :, None] < live_count[:, None, None])).astype(jnp.float32)
    summed = jnp.einsum("hlr,hlic->ric", select, terms, precision=lax.Precision.HIGHEST)
    return summed.reshape(GBLK * BLK, EXC)


def reference(retarded, block_row, block_count, send_pick, history, incident, self_block, sheet_diag):
    past_list = history
    results = []
    self_groups = self_block.astype(jnp.float32).reshape(GROUPS, GROUP_ROWS, GROUP_ROWS)
    for time_step in range(STEPS):
        def per_section(running, section):
            weights, row_list, live_count, picked, current = section
            weights = weights.reshape(GROUPS, GROUPS, LPG, BLK, BLK)
            row_list = row_list.reshape(GROUPS, GROUPS, LPG)
            live_count = live_count.reshape(GROUPS, GROUPS)
            reader_picks = jnp.transpose(picked)

            def per_group(inputs):
                return section_term(inputs[0], inputs[1], inputs[2], inputs[3], current)

            partial_value = lax.map(per_group, (weights, row_list, live_count, reader_picks))
            return running + partial_value.reshape(UNKNOWNS, EXC), None

        total_field, unused = lax.scan(per_section, jnp.zeros((UNKNOWNS, EXC), jnp.float32),
                                       (retarded, block_row, block_count, send_pick, past_list))
        driving = incident[time_step].astype(jnp.float32) - total_field
        diagonal = sheet_diag[:, None]
        iterate = driving / diagonal
        for sweep in range(ITERS):
            iterate_groups = iterate.astype(jnp.bfloat16).astype(jnp.float32).reshape(GROUPS, GROUP_ROWS, EXC)
            coupled = jnp.einsum("gij,gjc->gic", self_groups, iterate_groups, precision=lax.Precision.HIGHEST)
            iterate = (driving - coupled.reshape(UNKNOWNS, EXC)) / diagonal
        current = iterate.astype(jnp.bfloat16)
        results.append(current)
        past_list = jnp.concatenate([current[None], past_list[:-1]], axis=0)
    return jnp.stack(results)
```

```python
import jax
import jax.numpy as jnp
from jax import lax
from jax.experimental import pallas as pl
from jax.experimental.pallas import tpu as pltpu
from jax.sharding import PartitionSpec as P

STEPS = 4
ITERS = 3
SIDE = 4
GROUPS = 16
DELAYS = 16
CHIPS = 8
BLK = 256
ROWS = 1024
COLS = 128
PLACES = 3
MESH = pl.DeviceIdType.MESH
OFFSETS = sorted(
    [(dx, dy) for dx in range(SIDE) for dy in range(SIDE) if (dx, dy) != (0, 0)],
    key=lambda o: -(min(o[0], SIDE - o[0]) + min(o[1], SIDE - o[1])),
)


def kernel(
    row_ref, count_ref, pick_ref, weights_hbm, history_hbm, incident_hbm, self_hbm, diag_ref, out_hbm,
    weights, dense, self_block, incident, held, source, staged, blocks, total, rdiag, driving, iterate,
    partial_out, pair_in, chip_in, currents,
    local_sem, block_send, block_recv, shift_send, shift_recv, pair_send, pair_recv,
    chip_send, chip_recv, cast_send, cast_recv, fan_send, fan_recv, out_sem,
):
    g = lax.axis_index("group")
    d = lax.axis_index("delay")
    x, y = g // SIDE, g % SIDE
    chip, core = d // 2, d % 2
    first = d == 0

    def peer(dx, dy):
        return ((x + dx) % SIDE) * SIDE + (y + dy) % SIDE

    local = [
        pltpu.make_async_copy(history_hbm, held.at[0], local_sem.at[0]),
        pltpu.make_async_copy(weights_hbm, weights.at[pl.ds(0, GROUPS * PLACES)], local_sem.at[1]),
        pltpu.make_async_copy(self_hbm, self_block, local_sem.at[2]),
        pltpu.make_async_copy(incident_hbm, incident, local_sem.at[3]),
    ]
    for copy in local:
        copy.start()

    barrier = pltpu.get_barrier_semaphore()
    for dx, dy in OFFSETS:
        pl.semaphore_signal(barrier, inc=1, device_id=(peer(dx, dy), d), device_id_type=MESH)

    @pl.when(first)
    def _():
        for z in range(1, CHIPS):
            pl.semaphore_signal(barrier, inc=1, device_id=(g, 2 * z), device_id_type=MESH)
        pl.semaphore_signal(barrier, inc=1, device_id=(g, 1), device_id_type=MESH)
        pl.semaphore_wait(barrier, 15 + CHIPS)

    @pl.when(jnp.logical_and(core == 0, d > 0))
    def _():
        for other in (0, d - 1, d + 1):
            pl.semaphore_signal(barrier, inc=1, device_id=(g, other), device_id_type=MESH)
        pl.semaphore_wait(barrier, 15 + 3)

    @pl.when(jnp.logical_and(core == 1, d < DELAYS - 1))
    def _():
        for other in (d - 1, d + 1):
            pl.semaphore_signal(barrier, inc=1, device_id=(g, other), device_id_type=MESH)
        pl.semaphore_wait(barrier, 15 + 2)

    @pl.when(d == DELAYS - 1)
    def _():
        pl.semaphore_signal(barrier, inc=1, device_id=(g, d - 1), device_id_type=MESH)
        pl.semaphore_wait(barrier, 15 + 1)

    def shift(n):
        return pltpu.make_async_remote_copy(
            src_ref=held.at[n], dst_ref=held.at[n + 1], send_sem=shift_send.at[n], recv_sem=shift_recv.at[n + 1],
            device_id=(g, d + 1), device_id_type=MESH,
        )

    def block_copy(n, dx, dy):
        h = peer(dx, dy)
        return pltpu.make_async_remote_copy(
            src_ref=staged.at[n, h], dst_ref=blocks.at[n, x, y],
            send_sem=block_send.at[n, h], recv_sem=block_recv.at[n, g],
            device_id=(h, d), device_id_type=MESH,
        )

    def block_arrival(n, hx, hy):
        return pltpu.make_async_remote_copy(
            src_ref=staged.at[n, 0], dst_ref=blocks.at[n, hx, hy],
            send_sem=block_send.at[n, 0], recv_sem=block_recv.at[n, hx * SIDE + hy],
            device_id=(peer(1, 0), d), device_id_type=MESH,
        )

    def send_blocks(n):
        source[...] = held[n]
        for dx, dy in OFFSETS:
            h = peer(dx, dy)
            staged[n, h] = source[pick_ref[g, h]]
            block_copy(n, dx, dy).start()
        blocks[n, x, y] = source[pick_ref[g, g]]

        @pl.when(jnp.logical_and(n < STEPS - 1, d < DELAYS - 1))
        def _():
            shift(n).start()

    def pair(n):
        return pltpu.make_async_remote_copy(
            src_ref=partial_out.at[n], dst_ref=pair_in.at[n], send_sem=pair_send.at[n], recv_sem=pair_recv.at[n],
            device_id=(g, d - 1), device_id_type=MESH,
        )

    def to_first(n):
        return pltpu.make_async_remote_copy(
            src_ref=partial_out.at[n], dst_ref=chip_in.at[n, chip], send_sem=chip_send.at[n],
            recv_sem=chip_recv.at[n, chip], device_id=(g, 0), device_id_type=MESH,
        )

    def from_chip(n, z):
        return pltpu.make_async_remote_copy(
            src_ref=partial_out.at[n], dst_ref=chip_in.at[n, z], send_sem=chip_send.at[n],
            recv_sem=chip_recv.at[n, z], device_id=(g, 2), device_id_type=MESH,
        )

    def cast(n, z):
        return pltpu.make_async_remote_copy(
            src_ref=currents.at[n], dst_ref=currents.at[n], send_sem=cast_send.at[n, z], recv_sem=cast_recv.at[n],
            device_id=(g, 2 * z), device_id_type=MESH,
        )

    def fan(n):
        return pltpu.make_async_remote_copy(
            src_ref=currents.at[n], dst_ref=currents.at[n], send_sem=fan_send.at[n], recv_sem=fan_recv.at[n],
            device_id=(g, d + 1), device_id_type=MESH,
        )

    def store(n):
        return pltpu.make_async_copy(currents.at[n], out_hbm.at[n], out_sem.at[n])

    local[0].wait()
    send_blocks(0)

    weights[GROUPS * PLACES] = jnp.zeros((BLK, BLK), weights.dtype)
    for i in range(SIDE * 2):
        rows = jnp.broadcast_to(diag_ref[i : i + 1, :], (COLS, COLS))
        rdiag[pl.ds(i * COLS, COLS), :] = 1.0 / jnp.transpose(rows)
    local[1].wait()

    def spread(hx, carry):
        for hy in range(SIDE):
            h = hx * SIDE + hy
            for r in range(SIDE):
                place = jnp.int32(GROUPS * PLACES)
                for l in range(PLACES):
                    hit = jnp.logical_and(row_ref[h, l] == r, l < count_ref[h])
                    place = jnp.where(hit, h * PLACES + l, place)
                dense[hx, pl.ds(r * BLK, BLK), pl.ds(hy * BLK, BLK)] = weights[place]
        return carry

    lax.fori_loop(0, SIDE, spread, 0)
    local[2].wait()
    local[3].wait()

    def step(n, carry):
        def chunk(c, carry):
            hx = (x + c) % SIDE
            for hy in range(SIDE):
                @pl.when(jnp.logical_not(jnp.logical_and(hx == x, hy == y)))
                def _():
                    block_arrival(n, hx, hy).wait_recv()

            @pl.when(jnp.logical_and(c == SIDE - 1, jnp.logical_and(d > 0, n < STEPS - 1)))
            def _():
                shift_in = pltpu.make_async_remote_copy(
                    src_ref=held.at[n], dst_ref=held.at[n + 1], send_sem=shift_send.at[n],
                    recv_sem=shift_recv.at[n + 1], device_id=(g, d - 1), device_id_type=MESH,
                )
                shift_in.wait_recv()
                send_blocks(n + 1)

            value = jnp.dot(
                dense[hx], blocks[n, hx].reshape(ROWS, COLS), preferred_element_type=jnp.float32
            )

            @pl.when(c == 0)
            def _():
                total[...] = value

            @pl.when(c > 0)
            def _():
                total[...] += value

            return carry

        lax.fori_loop(0, SIDE, chunk, 0)

        @pl.when(core == 1)
        def _():
            partial_out[n] = total[...].astype(jnp.bfloat16)
            pair(n).start()

        @pl.when(jnp.logical_and(core == 0, d > 0))
        def _():
            from_pair(n).wait_recv()
            partial_out[n] = (total[...] + pair_in[n].astype(jnp.float32)).astype(jnp.bfloat16)
            to_first(n).start()

        @pl.when(first)
        def _():
            from_pair(n).wait_recv()
            value = incident[n].astype(jnp.float32) - total[...] - pair_in[n].astype(jnp.float32)
            driving[...] = value

            def gather(z, carry):
                from_chip(n, z).wait_recv()
                driving[...] -= chip_in[n, z].astype(jnp.float32)
                return carry

            lax.fori_loop(1, CHIPS, gather, 0)
            iterate[...] = driving[...] * rdiag[...]

            def sweep(k, carry):
                coupled = jnp.dot(
                    self_block[...], iterate[...].astype(jnp.bfloat16), preferred_element_type=jnp.float32
                )
                iterate[...] = (driving[...] - coupled) * rdiag[...]
                return carry

            lax.fori_loop(0, ITERS, sweep, 0)
            current = iterate[...].astype(jnp.bfloat16)
            currents[n] = current

            @pl.when(n < STEPS - 1)
            def _():
                held[n + 1] = current.reshape(SIDE, BLK, COLS)
                send_blocks(n + 1)

            for z in (4, 3, 5, 2, 6, 1, 7):
                cast(n, z).start()
            fan(n).start()
            store(n).start()

        return carry

    def from_pair(n):
        return pltpu.make_async_remote_copy(
            src_ref=partial_out.at[n], dst_ref=pair_in.at[n], send_sem=pair_send.at[n], recv_sem=pair_recv.at[n],
            device_id=(g, d + 1), device_id_type=MESH,
        )

    lax.fori_loop(0, STEPS, step, 0)

    def finish(n, carry):
        @pl.when(jnp.logical_and(core == 0, d > 0))
        def _():
            cast_in = pltpu.make_async_remote_copy(
                src_ref=currents.at[n], dst_ref=currents.at[n], send_sem=cast_send.at[n, 0],
                recv_sem=cast_recv.at[n], device_id=(g, 0), device_id_type=MESH,
            )
            cast_in.wait_recv()
            fan(n).start()
            store(n).start()

        @pl.when(core == 1)
        def _():
            fan_in = pltpu.make_async_remote_copy(
                src_ref=currents.at[n], dst_ref=currents.at[n], send_sem=fan_send.at[n],
                recv_sem=fan_recv.at[n], device_id=(g, d - 1), device_id_type=MESH,
            )
            fan_in.wait_recv()
            store(n).start()

        return carry

    lax.fori_loop(0, STEPS, finish, 0)

    def drain(n, carry):
        for dx, dy in OFFSETS:
            block_copy(n, dx, dy).wait_send()

        @pl.when(jnp.logical_and(n < STEPS - 1, d < DELAYS - 1))
        def _():
            shift(n).wait_send()

        @pl.when(core == 1)
        def _():
            pair(n).wait_send()

        @pl.when(core == 0)
        def _():
            fan(n).wait_send()

        @pl.when(jnp.logical_and(core == 0, d > 0))
        def _():
            to_first(n).wait_send()

        @pl.when(first)
        def _():
            for z in range(1, CHIPS):
                cast(n, z).wait_send()

        store(n).wait()
        return carry

    lax.fori_loop(0, STEPS, drain, 0)


def local(retarded, block_row, block_count, send_pick, history, incident, self_block, sheet_diag):
    smem = pl.BlockSpec(memory_space=pltpu.SMEM)
    vmem = pl.BlockSpec(memory_space=pltpu.VMEM)
    hbm = pl.BlockSpec(memory_space=pl.ANY)
    bf16, f32 = jnp.bfloat16, jnp.float32
    dma = pltpu.SemaphoreType.DMA
    call = pl.pallas_call(
        kernel,
        out_shape=jax.ShapeDtypeStruct((STEPS, ROWS, COLS), bf16),
        in_specs=[smem, smem, smem, hbm, hbm, hbm, hbm, vmem],
        out_specs=hbm,
        scratch_shapes=[
            pltpu.VMEM((GROUPS * PLACES + 1, BLK, BLK), bf16),
            pltpu.VMEM((SIDE, ROWS, ROWS), bf16),
            pltpu.VMEM((ROWS, ROWS), bf16),
            pltpu.VMEM((STEPS, ROWS, COLS), bf16),
            pltpu.VMEM((STEPS, SIDE, BLK, COLS), bf16),
            pltpu.VMEM((SIDE, BLK, COLS), bf16),
            pltpu.VMEM((STEPS, GROUPS, BLK, COLS), bf16),
            pltpu.VMEM((STEPS, SIDE, SIDE, BLK, COLS), bf16),
            pltpu.VMEM((ROWS, COLS), f32),
            pltpu.VMEM((ROWS, COLS), f32),
            pltpu.VMEM((ROWS, COLS), f32),
            pltpu.VMEM((ROWS, COLS), f32),
            pltpu.VMEM((STEPS, ROWS, COLS), bf16),
            pltpu.VMEM((STEPS, ROWS, COLS), bf16),
            pltpu.VMEM((STEPS, CHIPS, ROWS, COLS), bf16),
            pltpu.VMEM((STEPS, ROWS, COLS), bf16),
            dma((4,)),
            dma((STEPS, GROUPS)), dma((STEPS, GROUPS)),
            dma((STEPS,)), dma((STEPS,)),
            dma((STEPS,)), dma((STEPS,)),
            dma((STEPS,)), dma((STEPS, CHIPS)),
            dma((STEPS, CHIPS)), dma((STEPS,)),
            dma((STEPS,)), dma((STEPS,)),
            dma((STEPS,)),
        ],
        compiler_params=pltpu.CompilerParams(
            collective_id=0, has_side_effects=True, vmem_limit_bytes=56 * 2**20
        ),
        cost_estimate=pl.CostEstimate(flops=8 * 10**9, bytes_accessed=12 * 10**6, transcendentals=0),
    )
    return call(
        block_row[0], block_count[0], send_pick[0],
        retarded.reshape(GROUPS * PLACES, BLK, BLK), history.reshape(SIDE, BLK, COLS),
        incident, self_block, sheet_diag.reshape(SIDE * 2, COLS),
    )


def solution(mesh):
    placed = (
        P("delay", "group", None, None, None),
        P("delay", "group", None),
        P("delay", "group"),
        P("delay", None, None),
        P("delay", "group", None),
        P(None, "group", None),
        P("group", None),
        P("group"),
    )
    return jax.shard_map(
        local, mesh=mesh, in_specs=placed, out_specs=P(None, "group", None), check_vma=False
    )
```

```python
import jax
import jax.numpy as jnp
from jax import lax
from jax.experimental import pallas as pl
from jax.experimental.pallas import tpu as pltpu
from jax.sharding import PartitionSpec as P

STEPS = 4
SIDE = 4
GROUPS = 16
DELAYS = 16
CHIPS = 8
BLK = 256
ROWS = 1024
COLS = 128
PLACES = 3
MESH = pl.DeviceIdType.MESH
HALF = ROWS // 2
PART = HALF // CHIPS
SLAB = ROWS // CHIPS
OFFSETS = [(dx, dy) for dx in (2, 1, 3, 0) for dy in (2, 1, 3, 0) if (dx, dy) != (0, 0)]


def kernel(
    row_ref, count_ref, pick_ref, weights_hbm, history_hbm, incident_hbm, self_hbm, diag_ref, out_hbm,
    weights, dense, self_block, ratio, power, incident, held, source, staged, blocks, total, rdiag,
    pair_out, pair_in, half_out, half_in, part_out, part_in, chunk_out, chunk_in, first_in, currents,
    local_sem, block_send, block_recv, shift_send, shift_recv, pair_send, pair_recv, half_send, half_recv,
    part_send, part_recv, chunk_send, chunk_recv, first_recv,
    cast_send, cast_recv, fan_send, fan_recv, out_sem, turn_sem,
):
    g = lax.axis_index("group")
    d = lax.axis_index("delay")
    x, y = g // SIDE, g % SIDE
    chip, core = d // 2, d % 2
    first = d == 0

    def peer(dx, dy):
        return ((x + dx) % SIDE) * SIDE + (y + dy) % SIDE

    local = [
        pltpu.make_async_copy(history_hbm, held.at[0], local_sem.at[0]),
        pltpu.make_async_copy(weights_hbm, weights.at[pl.ds(0, GROUPS * PLACES)], local_sem.at[1]),
        pltpu.make_async_copy(self_hbm, self_block, local_sem.at[2]),
        pltpu.make_async_copy(incident_hbm, incident, local_sem.at[3]),
    ]
    for copy in local:
        copy.start()

    barrier = pltpu.get_barrier_semaphore()
    for dx, dy in OFFSETS:
        pl.semaphore_signal(barrier, inc=1, device_id=(peer(dx, dy), d), device_id_type=MESH)

    @pl.when(first)
    def _():
        for other in range(1, DELAYS):
            pl.semaphore_signal(barrier, inc=1, device_id=(g, other), device_id_type=MESH)

    @pl.when(d == 1)
    def _():
        for other in (0, 2):
            pl.semaphore_signal(barrier, inc=1, device_id=(g, other), device_id_type=MESH)

    @pl.when(d > 1)
    def _():
        pl.semaphore_signal(barrier, inc=1, device_id=(g, 0), device_id_type=MESH)
        pl.semaphore_signal(barrier, inc=1, device_id=(g, d - 1), device_id_type=MESH)

        @pl.when(d < DELAYS - 1)
        def _():
            pl.semaphore_signal(barrier, inc=1, device_id=(g, d + 1), device_id_type=MESH)

        for j in range(1, CHIPS):
            @pl.when(j != chip)
            def _():
                pl.semaphore_signal(barrier, inc=1, device_id=(g, 2 * j + core), device_id_type=MESH)

    def enter():
        greeted = jnp.where(d == 0, 15, jnp.where(d == 1, 2, jnp.where(d == DELAYS - 1, 8, 9)))
        pl.semaphore_wait(barrier, 15 + greeted)

    def shift(n):
        return pltpu.make_async_remote_copy(
            src_ref=held.at[n], dst_ref=held.at[n + 1], send_sem=shift_send.at[n], recv_sem=shift_recv.at[n + 1],
            device_id=(g, d + 1), device_id_type=MESH,
        )

    def block_copy(n, dx, dy):
        h = peer(dx, dy)
        return pltpu.make_async_remote_copy(
            src_ref=staged.at[n, h], dst_ref=blocks.at[n, x, y],
            send_sem=block_send.at[n, h], recv_sem=block_recv.at[n, g],
            device_id=(h, d), device_id_type=MESH,
        )

    def block_arrival(n, hx, hy):
        return pltpu.make_async_remote_copy(
            src_ref=staged.at[n, 0], dst_ref=blocks.at[n, hx, hy],
            send_sem=block_send.at[n, 0], recv_sem=block_recv.at[n, hx * SIDE + hy],
            device_id=(peer(1, 0), d), device_id_type=MESH,
        )

    def pack(n):
        source[...] = held[n]
        for dx, dy in OFFSETS:
            h = peer(dx, dy)
            staged[n, h] = source[pick_ref[g, h]]
        blocks[n, x, y] = source[pick_ref[g, g]]

    def start_shift(n):
        @pl.when(jnp.logical_and(n < STEPS - 1, jnp.logical_and(d >= n, d < DELAYS - 1)))
        def _():
            shift(n).start()

    def send_blocks(n):
        source[...] = held[n]
        for dx, dy in OFFSETS:
            h = peer(dx, dy)
            staged[n, h] = source[pick_ref[g, h]]
            block_copy(n, dx, dy).start()
        blocks[n, x, y] = source[pick_ref[g, g]]

    def pair(n, target):
        return pltpu.make_async_remote_copy(
            src_ref=pair_out.at[n], dst_ref=pair_in.at[n], send_sem=pair_send.at[n], recv_sem=pair_recv.at[n],
            device_id=(g, target), device_id_type=MESH,
        )

    def half(n):
        return pltpu.make_async_remote_copy(
            src_ref=half_out.at[n], dst_ref=half_in.at[n], send_sem=half_send.at[n], recv_sem=half_recv.at[n],
            device_id=(g, d + 1 - 2 * core), device_id_type=MESH,
        )

    def part(n, j):
        return pltpu.make_async_remote_copy(
            src_ref=part_out.at[n, j], dst_ref=part_in.at[n, chip], send_sem=part_send.at[n, j],
            recv_sem=part_recv.at[n, chip], device_id=(g, 2 * j + core), device_id_type=MESH,
        )

    def part_arrival(n, j):
        return pltpu.make_async_remote_copy(
            src_ref=part_out.at[n, j], dst_ref=part_in.at[n, j], send_sem=part_send.at[n, j],
            recv_sem=part_recv.at[n, j], device_id=(g, 2 * j + core), device_id_type=MESH,
        )

    def part_first(n, c, z, target):
        return pltpu.make_async_remote_copy(
            src_ref=part_out.at[n, 0], dst_ref=first_in.at[n, c, z], send_sem=part_send.at[n, 0],
            recv_sem=first_recv.at[n, c, z], device_id=(g, target), device_id_type=MESH,
        )

    def chunk(n, c, z, target):
        return pltpu.make_async_remote_copy(
            src_ref=chunk_out.at[n], dst_ref=chunk_in.at[n, c, z], send_sem=chunk_send.at[n],
            recv_sem=chunk_recv.at[n, c, z], device_id=(g, target), device_id_type=MESH,
        )

    def cast(n, k, j, slot):
        rows = pl.ds(k * SLAB, SLAB)
        return pltpu.make_async_remote_copy(
            src_ref=currents.at[n, rows], dst_ref=currents.at[n, rows], send_sem=cast_send.at[n, slot],
            recv_sem=cast_recv.at[n, k], device_id=(g, 2 * j), device_id_type=MESH,
        )

    def fan(n, k, target):
        rows = pl.ds(k * SLAB, SLAB)
        return pltpu.make_async_remote_copy(
            src_ref=currents.at[n, rows], dst_ref=currents.at[n, rows], send_sem=fan_send.at[n, k],
            recv_sem=fan_recv.at[n, k], device_id=(g, target), device_id_type=MESH,
        )

    def cast_all(n, j):
        return pltpu.make_async_remote_copy(
            src_ref=currents.at[n], dst_ref=currents.at[n], send_sem=cast_send.at[n, j],
            recv_sem=cast_recv.at[n, 0], device_id=(g, 2 * j), device_id_type=MESH,
        )

    def fan_all(n, target):
        return pltpu.make_async_remote_copy(
            src_ref=currents.at[n], dst_ref=currents.at[n], send_sem=fan_send.at[n, 0],
            recv_sem=fan_recv.at[n, 0], device_id=(g, target), device_id_type=MESH,
        )

    def store(n):
        return pltpu.make_async_copy(currents.at[n], out_hbm.at[n], out_sem.at[n])

    local[0].wait()
    pack(0)
    enter()
    for dx, dy in OFFSETS:
        block_copy(0, dx, dy).start()
    start_shift(0)

    weights[GROUPS * PLACES] = jnp.zeros((BLK, BLK), weights.dtype)
    for i in range(SIDE * 2):
        rows = jnp.broadcast_to(diag_ref[i : i + 1, :], (COLS, COLS))
        rdiag[pl.ds(i * COLS, COLS), :] = 1.0 / jnp.transpose(rows)
    local[1].wait()

    def spread(hx, carry):
        for hy in range(SIDE):
            h = hx * SIDE + hy
            for r in range(SIDE):
                place = jnp.int32(GROUPS * PLACES)
                for l in range(PLACES):
                    hit = jnp.logical_and(row_ref[l, 0, h] == r, l < count_ref[h])
                    place = jnp.where(hit, h * PLACES + l, place)
                dense[hx, pl.ds(r * BLK, BLK), pl.ds(hy * BLK, BLK)] = weights[place]
        return carry

    lax.fori_loop(0, SIDE, spread, 0)
    local[2].wait()
    local[3].wait()

    def fold_sweeps():
        wide = 2 * COLS

        def scaled(t, half):
            tile = pl.ds(pl.multiple_of(t * wide + half * COLS, COLS), COLS)
            return tile, self_block[:, tile].astype(jnp.float32) * rdiag[...]

        def scale(t, carry):
            for half in range(2):
                tile, value = scaled(t, half)
                ratio[:, tile] = value.astype(jnp.bfloat16)
            return carry

        lax.fori_loop(0, ROWS // wide, scale, 0)

        def fold(factor, result):
            def body(t, carry):
                both = pl.ds(pl.multiple_of(t * wide, wide), wide)
                product = jnp.dot(ratio[...], factor[:, both], preferred_element_type=jnp.float32)
                for half in range(2):
                    tile, value = scaled(t, half)
                    part = product[:, half * COLS : half * COLS + COLS]
                    result[:, tile] = (value - part).astype(jnp.bfloat16)
                return carry

            lax.fori_loop(0, ROWS // wide, body, 0)

        fold(ratio, power)
        fold(power, self_block)

    last = STEPS - 1

    def step(n, carry):
        def quarter(c, carry):
            hx = (x + jnp.where(c == 0, 2, jnp.where(c == 1, 3, jnp.where(c == 2, 1, 0)))) % SIDE
            for hy in range(SIDE):
                @pl.when(jnp.logical_not(jnp.logical_and(hx == x, hy == y)))
                def _():
                    block_arrival(n, hx, hy).wait_recv()

            @pl.when(jnp.logical_and(c == 0, jnp.logical_and(first, jnp.logical_or(n == 1, n == 2))))
            def _():
                pl.semaphore_signal(turn_sem, inc=1, device_id=(g, 1), device_id_type=MESH)

            @pl.when(c == 1)
            def _():
                @pl.when(jnp.logical_and(d > n, n < STEPS - 1))
                def _():
                    shift_in = pltpu.make_async_remote_copy(
                        src_ref=held.at[n], dst_ref=held.at[n + 1], send_sem=shift_send.at[n],
                        recv_sem=shift_recv.at[n + 1], device_id=(g, d - 1), device_id_type=MESH,
                    )
                    shift_in.wait_recv()
                    start_shift(n + 1)
                    send_blocks(n + 1)

            value = jnp.dot(
                dense[hx], blocks[n, hx].reshape(ROWS, COLS), preferred_element_type=jnp.float32
            )

            @pl.when(c == 0)
            def _():
                total[...] = value

            @pl.when(c > 0)
            def _():
                total[...] += value

            return carry

        lax.fori_loop(0, SIDE, quarter, 0)

        @pl.when(d == 1)
        def _():
            pair_out[n] = total[...].astype(jnp.bfloat16)
            pair(n, 0).start()

        @pl.when(d > 1)
        def _():
            mine = pl.ds(pl.multiple_of(core * HALF, HALF), HALF)
            other = pl.ds(pl.multiple_of(HALF - core * HALF, HALF), HALF)
            half_out[n] = total[other, :].astype(jnp.bfloat16)
            half(n).start()
            half(n).wait_recv()
            summed = total[mine, :] + half_in[n].astype(jnp.float32)
            total[mine, :] = summed
            part_out[n] = summed.astype(jnp.bfloat16).reshape(CHIPS, PART, COLS)
            for j in (4, 3, 5, 2, 6, 1, 7):
                @pl.when(j != chip)
                def _():
                    part(n, j).start()
            part_first(n, core, chip, 0).start()

            @pl.when(jnp.logical_and(d == 2, n == 2))
            def _():
                cast_all(0, 0).wait_recv()
                held[n + 1] = currents[0].reshape(SIDE, BLK, COLS)
                send_blocks(n + 1)

            place = pl.ds(pl.multiple_of(core * HALF + chip * PART, PART), PART)
            part_in[n, chip] = jnp.zeros((PART, COLS), jnp.bfloat16)
            for j in range(1, CHIPS):
                @pl.when(j != chip)
                def _():
                    part_arrival(n, j).wait_recv()
            value = total[place, :]
            for j in range(1, CHIPS):
                value += part_in[n, j].astype(jnp.float32)
            chunk_out[n] = value.astype(jnp.bfloat16)
            chunk(n, core, chip, 0).start()

        @pl.when(first)
        def _():
            pl.when(n == 0)(fold_sweeps)

            def arrive(z, carry):
                for c in range(2):
                    part_first(n, c, z, 2).wait_recv()
                    chunk(n, c, z, 2).wait_recv()
                return carry

            lax.fori_loop(1, CHIPS, arrive, 0)
            for c in range(2):
                value = first_in[n, c, 1].astype(jnp.float32)
                for z in range(2, CHIPS):
                    value += first_in[n, c, z].astype(jnp.float32)
                chunk_in[n, c, 0] = value.astype(jnp.bfloat16)
            pair(n, 1).wait_recv()
            value = incident[n].astype(jnp.float32) - chunk_in[n].reshape(ROWS, COLS).astype(jnp.float32)
            value = (value - pair_in[n].astype(jnp.float32) - total[...]) * rdiag[...]
            total[...] = value
            coupled = jnp.dot(self_block[...], value.astype(jnp.bfloat16), preferred_element_type=jnp.float32)
            current = (total[...] - coupled).astype(jnp.bfloat16)
            currents[n] = current

            @pl.when(n < STEPS - 1)
            def _():
                held[n + 1] = current.reshape(SIDE, BLK, COLS)
                send_blocks(n + 1)
                fan_all(n, 1).start()
                for j in (1, 4, 3, 5, 2, 6, 7):
                    cast_all(n, j).start()

            @pl.when(n == last)
            def _():
                for j in (4, 3, 5, 2, 6, 1, 7):
                    cast(last, j, j, j).start()
                for j in (4, 3, 5, 2, 6, 1, 7):
                    cast(last, 0, j, CHIPS + j).start()
                for k in range(CHIPS):
                    fan(last, k, 1).start()

            store(n).start()

        @pl.when(jnp.logical_and(d == 1, jnp.logical_or(n == 1, n == 2)))
        def _():
            fan_all(n - 1, 0).wait_recv()
            held[n + 1] = currents[n - 1].reshape(SIDE, BLK, COLS)
            pack(n + 1)
            pl.semaphore_wait(turn_sem, 1)
            for dx, dy in OFFSETS:
                block_copy(n + 1, dx, dy).start()

        return carry

    lax.fori_loop(0, STEPS, step, 0)

    def finish(n, carry):
        @pl.when(jnp.logical_and(core == 0, d > 0))
        def _():
            @pl.when(jnp.logical_not(jnp.logical_and(d == 2, n == 0)))
            def _():
                cast_all(n, 0).wait_recv()

            fan_all(n, d + 1).start()
            store(n).start()

        @pl.when(core == 1)
        def _():
            @pl.when(jnp.logical_or(d > 1, n == last - 1))
            def _():
                fan_all(n, d - 1).wait_recv()

            store(n).start()

        return carry

    lax.fori_loop(0, last, finish, 0)

    @pl.when(jnp.logical_and(core == 0, d > 0))
    def _():
        cast(last, chip, 0, 0).wait_recv()
        for j in range(1, CHIPS):
            to = (chip + j) % CHIPS

            @pl.when(to > 0)
            def _():
                cast(last, chip, to, to).start()
        fan(last, chip, d + 1).start()
        for j in range(1, CHIPS):
            k = (chip + j) % CHIPS
            cast(last, k, 0, 0).wait_recv()
            fan(last, k, d + 1).start()
        store(last).start()

    @pl.when(core == 1)
    def _():
        for k in range(CHIPS):
            fan(last, k, d - 1).wait_recv()
        store(last).start()

    def drain(n, carry):
        for dx, dy in OFFSETS:
            block_copy(n, dx, dy).wait_send()

        @pl.when(jnp.logical_and(n < STEPS - 1, jnp.logical_and(d >= n, d < DELAYS - 1)))
        def _():
            shift(n).wait_send()

        @pl.when(d == 1)
        def _():
            pair(n, 0).wait_send()

        @pl.when(d > 1)
        def _():
            half(n).wait_send()
            part_first(n, core, chip, 0).wait_send()
            chunk(n, core, chip, 0).wait_send()
            for j in range(1, CHIPS):
                @pl.when(j != chip)
                def _():
                    part(n, j).wait_send()

        @pl.when(jnp.logical_and(core == 0, n < last))
        def _():
            fan_all(n, d + 1).wait_send()

        @pl.when(jnp.logical_and(first, n < last))
        def _():
            for j in range(1, CHIPS):
                cast_all(n, j).wait_send()

        store(n).wait()
        return carry

    lax.fori_loop(0, STEPS, drain, 0)

    @pl.when(core == 0)
    def _():
        for k in range(CHIPS):
            fan(last, k, d + 1).wait_send()
        for j in range(1, CHIPS):
            @pl.when(j != chip)
            def _():
                cast(last, chip, j, j).wait_send()

    @pl.when(first)
    def _():
        for j in range(1, CHIPS):
            cast(last, 0, j, CHIPS + j).wait_send()


def local(retarded, block_row, block_count, send_pick, history, incident, self_block, sheet_diag):
    smem = pl.BlockSpec(memory_space=pltpu.SMEM)
    vmem = pl.BlockSpec(memory_space=pltpu.VMEM)
    hbm = pl.BlockSpec(memory_space=pl.ANY)
    bf16, f32 = jnp.bfloat16, jnp.float32
    dma = pltpu.SemaphoreType.DMA
    call = pl.pallas_call(
        kernel,
        out_shape=jax.ShapeDtypeStruct((STEPS, ROWS, COLS), bf16),
        in_specs=[smem, smem, smem, hbm, hbm, hbm, hbm, vmem],
        out_specs=hbm,
        scratch_shapes=[
            pltpu.VMEM((GROUPS * PLACES + 1, BLK, BLK), bf16),
            pltpu.VMEM((SIDE, ROWS, ROWS), bf16),
            pltpu.VMEM((ROWS, ROWS), bf16),
            pltpu.VMEM((ROWS, ROWS), bf16),
            pltpu.VMEM((ROWS, ROWS), bf16),
            pltpu.VMEM((STEPS, ROWS, COLS), bf16),
            pltpu.VMEM((STEPS, SIDE, BLK, COLS), bf16),
            pltpu.VMEM((SIDE, BLK, COLS), bf16),
            pltpu.VMEM((STEPS, GROUPS, BLK, COLS), bf16),
            pltpu.VMEM((STEPS, SIDE, SIDE, BLK, COLS), bf16),
            pltpu.VMEM((ROWS, COLS), f32),
            pltpu.VMEM((ROWS, COLS), f32),
            pltpu.VMEM((STEPS, ROWS, COLS), bf16),
            pltpu.VMEM((STEPS, ROWS, COLS), bf16),
            pltpu.VMEM((STEPS, HALF, COLS), bf16),
            pltpu.VMEM((STEPS, HALF, COLS), bf16),
            pltpu.VMEM((STEPS, CHIPS, PART, COLS), bf16),
            pltpu.VMEM((STEPS, CHIPS, PART, COLS), bf16),
            pltpu.VMEM((STEPS, PART, COLS), bf16),
            pltpu.VMEM((STEPS, 2, CHIPS, PART, COLS), bf16),
            pltpu.VMEM((STEPS, 2, CHIPS, PART, COLS), bf16),
            pltpu.VMEM((STEPS, ROWS, COLS), bf16),
            dma((4,)),
            dma((STEPS, GROUPS)), dma((STEPS, GROUPS)),
            dma((STEPS,)), dma((STEPS,)),
            dma((STEPS,)), dma((STEPS,)),
            dma((STEPS,)), dma((STEPS,)),
            dma((STEPS, CHIPS)), dma((STEPS, CHIPS)),
            dma((STEPS,)), dma((STEPS, 2, CHIPS)), dma((STEPS, 2, CHIPS)),
            dma((STEPS, 2 * CHIPS)), dma((STEPS, CHIPS)),
            dma((STEPS, CHIPS)), dma((STEPS, CHIPS)),
            dma((STEPS,)),
            pltpu.SemaphoreType.REGULAR,
        ],
        compiler_params=pltpu.CompilerParams(
            collective_id=0, has_side_effects=True, vmem_limit_bytes=56 * 2**20
        ),
        cost_estimate=pl.CostEstimate(flops=8 * 10**9, bytes_accessed=12 * 10**6, transcendentals=0),
    )
    return call(
        jnp.transpose(block_row, (2, 0, 1)), block_count[0], send_pick[0],
        retarded.reshape(GROUPS * PLACES, BLK, BLK), history.reshape(SIDE, BLK, COLS),
        incident, self_block, sheet_diag.reshape(SIDE * 2, COLS),
    )


def solution(mesh):
    placed = (
        P("delay", "group", None, None, None),
        P("delay", "group", None),
        P("delay", "group"),
        P("delay", None, None),
        P("delay", "group", None),
        P(None, "group", None),
        P("group", None),
        P("group"),
    )
    return jax.shard_map(
        local, mesh=mesh, in_specs=placed, out_specs=P(None, "group", None), check_vma=False
    )
```

```python
import jax
import jax.numpy as jnp
from jax import lax
from jax.experimental import pallas as pl
from jax.experimental.pallas import tpu as pltpu
from jax.sharding import PartitionSpec as P

STEPS = 4
SIDE = 4
GROUPS = 16
DELAYS = 16
CHIPS = 8
BLK = 256
ROWS = 1024
COLS = 128
PLACES = 3
MESH = pl.DeviceIdType.MESH
HALF = ROWS // 2
PART = HALF // CHIPS
SLAB = ROWS // CHIPS
OFFSETS = [(dx, dy) for dx in (2, 1, 3, 0) for dy in (2, 1, 3, 0) if (dx, dy) != (0, 0)]


def kernel(
    row_ref, count_ref, pick_ref, weights_hbm, history_hbm, incident_hbm, self_hbm, diag_ref, out_hbm,
    weights, dense, self_block, ratio, power, incident, held, source, staged, blocks, total, rdiag,
    pair_out, pair_in, half_out, half_in, part_out, part_in, chunk_out, chunk_in, first_in, currents,
    local_sem, block_send, block_recv, shift_send, shift_recv, pair_send, pair_recv, half_send, half_recv,
    part_send, part_recv, chunk_send, chunk_recv, first_recv,
    cast_send, cast_recv, fan_send, fan_recv, out_sem, turn_sem,
):
    g = lax.axis_index("group")
    d = lax.axis_index("delay")
    x, y = g // SIDE, g % SIDE
    chip, core = d // 2, d % 2
    first = d == 0

    def peer(dx, dy):
        return ((x + dx) % SIDE) * SIDE + (y + dy) % SIDE

    local = [
        pltpu.make_async_copy(history_hbm, held.at[0], local_sem.at[0]),
        pltpu.make_async_copy(weights_hbm, weights.at[pl.ds(0, GROUPS * PLACES)], local_sem.at[1]),
        pltpu.make_async_copy(self_hbm, self_block, local_sem.at[2]),
        pltpu.make_async_copy(incident_hbm, incident, local_sem.at[3]),
    ]
    for copy in local:
        copy.start()

    barrier = pltpu.get_barrier_semaphore()
    for dx, dy in OFFSETS:
        pl.semaphore_signal(barrier, inc=1, device_id=(peer(dx, dy), d), device_id_type=MESH)

    @pl.when(first)
    def _():
        for other in range(1, DELAYS):
            pl.semaphore_signal(barrier, inc=1, device_id=(g, other), device_id_type=MESH)

    @pl.when(d == 1)
    def _():
        for other in (0, 2):
            pl.semaphore_signal(barrier, inc=1, device_id=(g, other), device_id_type=MESH)

    @pl.when(d > 1)
    def _():
        pl.semaphore_signal(barrier, inc=1, device_id=(g, 0), device_id_type=MESH)
        pl.semaphore_signal(barrier, inc=1, device_id=(g, d - 1), device_id_type=MESH)

        @pl.when(d < DELAYS - 1)
        def _():
            pl.semaphore_signal(barrier, inc=1, device_id=(g, d + 1), device_id_type=MESH)

        for j in range(1, CHIPS):
            @pl.when(j != chip)
            def _():
                pl.semaphore_signal(barrier, inc=1, device_id=(g, 2 * j + core), device_id_type=MESH)

    def enter():
        greeted = jnp.where(d == 0, 15, jnp.where(d == 1, 2, jnp.where(d == DELAYS - 1, 8, 9)))
        pl.semaphore_wait(barrier, 15 + greeted)

    def shift(n):
        return pltpu.make_async_remote_copy(
            src_ref=held.at[n], dst_ref=held.at[n + 1], send_sem=shift_send.at[n], recv_sem=shift_recv.at[n + 1],
            device_id=(g, d + 1), device_id_type=MESH,
        )

    def block_copy(n, dx, dy):
        h = peer(dx, dy)
        return pltpu.make_async_remote_copy(
            src_ref=staged.at[n, h], dst_ref=blocks.at[n, x, y],
            send_sem=block_send.at[n], recv_sem=block_recv.at[n, x],
            device_id=(h, d), device_id_type=MESH,
        )

    def all_sent(ref, sem):
        pltpu.make_async_remote_copy(
            src_ref=ref, dst_ref=ref, send_sem=sem, recv_sem=sem, device_id=(g, d + 1 - 2 * core), device_id_type=MESH,
        ).wait_send()

    def all_come(ref, sem):
        pltpu.make_async_remote_copy(
            src_ref=ref, dst_ref=ref, send_sem=sem, recv_sem=sem, device_id=(g, d + 1 - 2 * core), device_id_type=MESH,
        ).wait_recv()

    def pack(n):
        source[...] = held[n]
        for dx, dy in OFFSETS:
            h = peer(dx, dy)
            staged[n, h] = source[pick_ref[g, h]]
        blocks[n, x, y] = source[pick_ref[g, g]]

    def start_shift(n):
        @pl.when(jnp.logical_and(n < STEPS - 1, jnp.logical_and(d >= n, d < DELAYS - 1)))
        def _():
            shift(n).start()

    def send_blocks(n):
        source[...] = held[n]
        for dx, dy in OFFSETS:
            h = peer(dx, dy)
            staged[n, h] = source[pick_ref[g, h]]
            block_copy(n, dx, dy).start()
        blocks[n, x, y] = source[pick_ref[g, g]]

    def pair(n, target):
        return pltpu.make_async_remote_copy(
            src_ref=pair_out.at[n], dst_ref=pair_in.at[n], send_sem=pair_send.at[0], recv_sem=pair_recv.at[n],
            device_id=(g, target), device_id_type=MESH,
        )

    def half(n):
        return pltpu.make_async_remote_copy(
            src_ref=half_out.at[n], dst_ref=half_in.at[n], send_sem=half_send.at[0], recv_sem=half_recv.at[n],
            device_id=(g, d + 1 - 2 * core), device_id_type=MESH,
        )

    def part(n, j):
        return pltpu.make_async_remote_copy(
            src_ref=part_out.at[n, j], dst_ref=part_in.at[n, chip], send_sem=part_send.at[n],
            recv_sem=part_recv.at[n], device_id=(g, 2 * j + core), device_id_type=MESH,
        )

    def part_first(n, c, z, target):
        return pltpu.make_async_remote_copy(
            src_ref=part_out.at[n, 0], dst_ref=first_in.at[n, c, z], send_sem=part_send.at[n],
            recv_sem=first_recv.at[n], device_id=(g, target), device_id_type=MESH,
        )

    def chunk(n, c, z, target):
        return pltpu.make_async_remote_copy(
            src_ref=chunk_out.at[n], dst_ref=chunk_in.at[n, c, z], send_sem=chunk_send.at[0],
            recv_sem=chunk_recv.at[n], device_id=(g, target), device_id_type=MESH,
        )

    last = STEPS - 1

    def cast(k, j):
        rows = pl.ds(k * SLAB, SLAB)
        return pltpu.make_async_remote_copy(
            src_ref=currents.at[last, rows], dst_ref=currents.at[last, rows], send_sem=cast_send.at[last],
            recv_sem=cast_recv.at[last + k], device_id=(g, 2 * j), device_id_type=MESH,
        )

    def fan(k, target):
        rows = pl.ds(k * SLAB, SLAB)
        return pltpu.make_async_remote_copy(
            src_ref=currents.at[last, rows], dst_ref=currents.at[last, rows], send_sem=fan_send.at[last],
            recv_sem=fan_recv.at[last], device_id=(g, target), device_id_type=MESH,
        )

    def cast_all(n, j):
        return pltpu.make_async_remote_copy(
            src_ref=currents.at[n], dst_ref=currents.at[n], send_sem=cast_send.at[n],
            recv_sem=cast_recv.at[n], device_id=(g, 2 * j), device_id_type=MESH,
        )

    def fan_all(n, target):
        return pltpu.make_async_remote_copy(
            src_ref=currents.at[n], dst_ref=currents.at[n], send_sem=fan_send.at[n],
            recv_sem=fan_recv.at[n], device_id=(g, target), device_id_type=MESH,
        )

    def store(n):
        return pltpu.make_async_copy(currents.at[n], out_hbm.at[n], out_sem.at[0])

    local[0].wait()
    pack(0)
    enter()
    for dx, dy in OFFSETS:
        block_copy(0, dx, dy).start()
    start_shift(0)

    weights[GROUPS * PLACES] = jnp.zeros((BLK, BLK), weights.dtype)
    for i in range(SIDE * 2):
        rows = jnp.broadcast_to(diag_ref[i : i + 1, :], (COLS, COLS))
        rdiag[pl.ds(i * COLS, COLS), :] = 1.0 / jnp.transpose(rows)
    local[1].wait()

    def spread(hx, carry):
        for hy in range(SIDE):
            h = hx * SIDE + hy
            for r in range(SIDE):
                place = jnp.int32(GROUPS * PLACES)
                for l in range(PLACES):
                    hit = jnp.logical_and(row_ref[l, 0, h] == r, l < count_ref[h])
                    place = jnp.where(hit, h * PLACES + l, place)
                dense[hx, pl.ds(r * BLK, BLK), pl.ds(hy * BLK, BLK)] = weights[place]
        return carry

    lax.fori_loop(0, SIDE, spread, 0)
    local[2].wait()
    local[3].wait()

    def fold_sweeps():
        wide = 2 * COLS

        def scaled(t, half):
            tile = pl.ds(pl.multiple_of(t * wide + half * COLS, COLS), COLS)
            return tile, self_block[:, tile].astype(jnp.float32) * rdiag[...]

        def scale(t, carry):
            for half in range(2):
                tile, value = scaled(t, half)
                ratio[:, tile] = value.astype(jnp.bfloat16)
            return carry

        lax.fori_loop(0, ROWS // wide, scale, 0)

        def fold(factor, result):
            def body(t, carry):
                both = pl.ds(pl.multiple_of(t * wide, wide), wide)
                product = jnp.dot(ratio[...], factor[:, both], preferred_element_type=jnp.float32)
                for half in range(2):
                    tile, value = scaled(t, half)
                    part = product[:, half * COLS : half * COLS + COLS]
                    result[:, tile] = (value - part).astype(jnp.bfloat16)
                return carry

            lax.fori_loop(0, ROWS // wide, body, 0)

        fold(ratio, power)
        fold(power, self_block)

    def step(n, carry):
        def quarter(c, carry):
            hx = (x + jnp.where(c == 0, 2, jnp.where(c == 1, 3, jnp.where(c == 2, 1, 0)))) % SIDE
            @pl.when(hx == x)
            def _():
                all_come(blocks.at[n, hx, pl.ds(0, SIDE - 1)], block_recv.at[n, hx])

            @pl.when(hx != x)
            def _():
                all_come(blocks.at[n, hx], block_recv.at[n, hx])

            @pl.when(jnp.logical_and(c == 0, jnp.logical_and(first, jnp.logical_or(n == 1, n == 2))))
            def _():
                pl.semaphore_signal(turn_sem, inc=1, device_id=(g, 1), device_id_type=MESH)

            @pl.when(c == 1)
            def _():
                @pl.when(jnp.logical_and(d > n, n < STEPS - 1))
                def _():
                    shift_in = pltpu.make_async_remote_copy(
                        src_ref=held.at[n], dst_ref=held.at[n + 1], send_sem=shift_send.at[n],
                        recv_sem=shift_recv.at[n + 1], device_id=(g, d - 1), device_id_type=MESH,
                    )
                    shift_in.wait_recv()
                    start_shift(n + 1)
                    send_blocks(n + 1)

            value = jnp.dot(
                dense[hx], blocks[n, hx].reshape(ROWS, COLS), preferred_element_type=jnp.float32
            )

            @pl.when(c == 0)
            def _():
                total[...] = value

            @pl.when(c > 0)
            def _():
                total[...] += value

            return carry

        lax.fori_loop(0, SIDE, quarter, 0)

        @pl.when(d == 1)
        def _():
            pair_out[n] = total[...].astype(jnp.bfloat16)
            pair(n, 0).start()

        @pl.when(d > 1)
        def _():
            mine = pl.ds(pl.multiple_of(core * HALF, HALF), HALF)
            other = pl.ds(pl.multiple_of(HALF - core * HALF, HALF), HALF)
            half_out[n] = total[other, :].astype(jnp.bfloat16)
            half(n).start()
            half(n).wait_recv()
            summed = total[mine, :] + half_in[n].astype(jnp.float32)
            total[mine, :] = summed
            part_out[n] = summed.astype(jnp.bfloat16).reshape(CHIPS, PART, COLS)
            for j in (4, 3, 5, 2, 6, 1, 7):
                @pl.when(j != chip)
                def _():
                    part(n, j).start()
            part_first(n, core, chip, 0).start()

            @pl.when(jnp.logical_and(d == 2, n == 2))
            def _():
                cast_all(0, 0).wait_recv()
                held[n + 1] = currents[0].reshape(SIDE, BLK, COLS)
                send_blocks(n + 1)

            place = pl.ds(pl.multiple_of(core * HALF + chip * PART, PART), PART)
            all_come(part_in.at[n, pl.ds(0, CHIPS - 2)], part_recv.at[n])
            part_in[n, chip] = jnp.zeros((PART, COLS), jnp.bfloat16)
            value = total[place, :]
            for j in range(1, CHIPS):
                value += part_in[n, j].astype(jnp.float32)
            chunk_out[n] = value.astype(jnp.bfloat16)
            chunk(n, core, chip, 0).start()

        @pl.when(first)
        def _():
            pl.when(n == 0)(fold_sweeps)

            all_come(first_in.at[n, :, pl.ds(0, CHIPS - 1)], first_recv.at[n])
            all_come(chunk_in.at[n, :, pl.ds(0, CHIPS - 1)], chunk_recv.at[n])
            for c in range(2):
                value = first_in[n, c, 1].astype(jnp.float32)
                for z in range(2, CHIPS):
                    value += first_in[n, c, z].astype(jnp.float32)
                chunk_in[n, c, 0] = value.astype(jnp.bfloat16)
            pair(n, 1).wait_recv()
            value = incident[n].astype(jnp.float32) - chunk_in[n].reshape(ROWS, COLS).astype(jnp.float32)
            value = (value - pair_in[n].astype(jnp.float32) - total[...]) * rdiag[...]
            total[...] = value
            coupled = jnp.dot(self_block[...], value.astype(jnp.bfloat16), preferred_element_type=jnp.float32)
            current = (total[...] - coupled).astype(jnp.bfloat16)
            currents[n] = current

            @pl.when(n < STEPS - 1)
            def _():
                held[n + 1] = current.reshape(SIDE, BLK, COLS)
                send_blocks(n + 1)
                fan_all(n, 1).start()
                for j in (1, 4, 3, 5, 2, 6, 7):
                    cast_all(n, j).start()

            @pl.when(n == last)
            def _():
                for j in (4, 3, 5, 2, 6, 1, 7):
                    cast(j, j).start()
                for j in (4, 3, 5, 2, 6, 1, 7):
                    cast(0, j).start()
                for k in range(CHIPS):
                    fan(k, 1).start()

            store(n).start()

        @pl.when(jnp.logical_and(d == 1, jnp.logical_or(n == 1, n == 2)))
        def _():
            fan_all(n - 1, 0).wait_recv()
            held[n + 1] = currents[n - 1].reshape(SIDE, BLK, COLS)
            pack(n + 1)
            pl.semaphore_wait(turn_sem, 1)
            for dx, dy in OFFSETS:
                block_copy(n + 1, dx, dy).start()

        return carry

    lax.fori_loop(0, STEPS, step, 0)

    def finish(n, carry):
        @pl.when(jnp.logical_and(core == 0, d > 0))
        def _():
            @pl.when(jnp.logical_not(jnp.logical_and(d == 2, n == 0)))
            def _():
                cast_all(n, 0).wait_recv()

            fan_all(n, d + 1).start()
            store(n).start()

        @pl.when(core == 1)
        def _():
            @pl.when(jnp.logical_or(d > 1, n == last - 1))
            def _():
                fan_all(n, d - 1).wait_recv()

            store(n).start()

        return carry

    lax.fori_loop(0, last, finish, 0)

    @pl.when(jnp.logical_and(core == 0, d > 0))
    def _():
        cast(chip, 0).wait_recv()
        for j in range(1, CHIPS):
            to = (chip + j) % CHIPS

            @pl.when(to > 0)
            def _():
                cast(chip, to).start()
        fan(chip, d + 1).start()
        for j in range(1, CHIPS):
            k = (chip + j) % CHIPS
            cast(k, 0).wait_recv()
            fan(k, d + 1).start()
        store(last).start()

    @pl.when(core == 1)
    def _():
        all_come(currents.at[last], fan_recv.at[last])
        store(last).start()

    def drain(n, carry):
        all_sent(staged.at[n, pl.ds(0, GROUPS - 1)], block_send.at[n])

        @pl.when(jnp.logical_and(n < STEPS - 1, jnp.logical_and(d >= n, d < DELAYS - 1)))
        def _():
            shift(n).wait_send()

        @pl.when(d > 1)
        def _():
            all_sent(part_out.at[n, pl.ds(0, CHIPS - 1)], part_send.at[n])

        @pl.when(core == 0)
        def _():
            all_sent(currents.at[n], fan_send.at[n])

        @pl.when(jnp.logical_and(first, n < last))
        def _():
            all_sent(weights.at[pl.ds(0, 2 * CHIPS - 2)], cast_send.at[n])

        return carry

    lax.fori_loop(0, STEPS, drain, 0)

    @pl.when(d == 1)
    def _():
        all_sent(pair_out, pair_send.at[0])

    @pl.when(d > 1)
    def _():
        all_sent(half_out, half_send.at[0])
        all_sent(chunk_out, chunk_send.at[0])

    @pl.when(first)
    def _():
        all_sent(staged.at[0, pl.ds(0, CHIPS - 1)], cast_send.at[last])

    @pl.when(jnp.logical_and(core == 0, d > 0))
    def _():
        all_sent(staged.at[0, pl.ds(0, CHIPS // 2 - 1)], cast_send.at[last])

    pltpu.make_async_copy(currents, out_hbm, out_sem.at[0]).wait()


def local(retarded, block_row, block_count, send_pick, history, incident, self_block, sheet_diag):
    smem = pl.BlockSpec(memory_space=pltpu.SMEM)
    vmem = pl.BlockSpec(memory_space=pltpu.VMEM)
    hbm = pl.BlockSpec(memory_space=pl.ANY)
    bf16, f32 = jnp.bfloat16, jnp.float32
    dma = pltpu.SemaphoreType.DMA
    call = pl.pallas_call(
        kernel,
        out_shape=jax.ShapeDtypeStruct((STEPS, ROWS, COLS), bf16),
        in_specs=[smem, smem, smem, hbm, hbm, hbm, hbm, vmem],
        out_specs=hbm,
        scratch_shapes=[
            pltpu.VMEM((GROUPS * PLACES + 1, BLK, BLK), bf16),
            pltpu.VMEM((SIDE, ROWS, ROWS), bf16),
            pltpu.VMEM((ROWS, ROWS), bf16),
            pltpu.VMEM((ROWS, ROWS), bf16),
            pltpu.VMEM((ROWS, ROWS), bf16),
            pltpu.VMEM((STEPS, ROWS, COLS), bf16),
            pltpu.VMEM((STEPS, SIDE, BLK, COLS), bf16),
            pltpu.VMEM((SIDE, BLK, COLS), bf16),
            pltpu.VMEM((STEPS, GROUPS, BLK, COLS), bf16),
            pltpu.VMEM((STEPS, SIDE, SIDE, BLK, COLS), bf16),
            pltpu.VMEM((ROWS, COLS), f32),
            pltpu.VMEM((ROWS, COLS), f32),
            pltpu.VMEM((STEPS, ROWS, COLS), bf16),
            pltpu.VMEM((STEPS, ROWS, COLS), bf16),
            pltpu.VMEM((STEPS, HALF, COLS), bf16),
            pltpu.VMEM((STEPS, HALF, COLS), bf16),
            pltpu.VMEM((STEPS, CHIPS, PART, COLS), bf16),
            pltpu.VMEM((STEPS, CHIPS, PART, COLS), bf16),
            pltpu.VMEM((STEPS, PART, COLS), bf16),
            pltpu.VMEM((STEPS, 2, CHIPS, PART, COLS), bf16),
            pltpu.VMEM((STEPS, 2, CHIPS, PART, COLS), bf16),
            pltpu.VMEM((STEPS, ROWS, COLS), bf16),
            dma((4,)),
            dma((STEPS,)), dma((STEPS, SIDE)),
            dma((STEPS,)), dma((STEPS,)),
            dma((1,)), dma((STEPS,)),
            dma((1,)), dma((STEPS,)),
            dma((STEPS,)), dma((STEPS,)),
            dma((1,)), dma((STEPS,)), dma((STEPS,)),
            dma((STEPS,)), dma((STEPS + CHIPS,)),
            dma((STEPS,)), dma((STEPS,)),
            dma((1,)),
            pltpu.SemaphoreType.REGULAR,
        ],
        compiler_params=pltpu.CompilerParams(
            collective_id=0, has_side_effects=True, vmem_limit_bytes=56 * 2**20
        ),
        cost_estimate=pl.CostEstimate(flops=8 * 10**9, bytes_accessed=12 * 10**6, transcendentals=0),
    )
    return call(
        jnp.transpose(block_row, (2, 0, 1)), block_count[0], send_pick[0],
        retarded.reshape(GROUPS * PLACES, BLK, BLK), history.reshape(SIDE, BLK, COLS),
        incident, self_block, sheet_diag.reshape(SIDE * 2, COLS),
    )


def solution(mesh):
    placed = (
        P("delay", "group", None, None, None),
        P("delay", "group", None),
        P("delay", "group"),
        P("delay", None, None),
        P("delay", "group", None),
        P(None, "group", None),
        P("group", None),
        P("group"),
    )
    return jax.shard_map(
        local, mesh=mesh, in_specs=placed, out_specs=P(None, "group", None), check_vma=False
    )
```

```python
import jax
import jax.numpy as jnp
from jax import lax
from jax.experimental import pallas as pl
from jax.experimental.pallas import tpu as pltpu
from jax.sharding import PartitionSpec as P

STEPS = 4
SIDE = 4
GROUPS = 16
DELAYS = 16
CHIPS = 8
BLK = 256
ROWS = 1024
COLS = 128
PLACES = 3
MESH = pl.DeviceIdType.MESH
HALF = ROWS // 2
PART = HALF // CHIPS
SLAB = ROWS // CHIPS
OFFSETS = [(dx, dy) for dx in (2, 1, 3, 0) for dy in (2, 1, 3, 0) if (dx, dy) != (0, 0)]


def kernel(
    row_ref, count_ref, pick_ref, weights_hbm, history_hbm, incident_hbm, self_hbm, diag_ref, out_hbm,
    weights, dense, self_block, ratio, power, incident, held, source, staged, blocks, total, rdiag,
    pair_out, pair_in, half_out, half_in, part_out, part_in, chunk_out, chunk_in, first_in, currents,
    local_sem, block_send, block_recv, shift_send, shift_recv, pair_send, pair_recv, half_send, half_recv,
    part_send, part_recv, chunk_send, chunk_recv, first_recv,
    cast_send, cast_recv, fan_send, fan_recv, out_sem, turn_sem,
):
    g = lax.axis_index("group")
    d = lax.axis_index("delay")
    x, y = g // SIDE, g % SIDE
    chip, core = d // 2, d % 2
    first = d == 0

    def peer(dx, dy):
        return ((x + dx) % SIDE) * SIDE + (y + dy) % SIDE

    local = [
        pltpu.make_async_copy(history_hbm, held.at[0], local_sem.at[0]),
        pltpu.make_async_copy(weights_hbm, weights.at[pl.ds(0, GROUPS * PLACES)], local_sem.at[1]),
        pltpu.make_async_copy(self_hbm, self_block, local_sem.at[2]),
        pltpu.make_async_copy(incident_hbm, incident, local_sem.at[3]),
    ]
    for copy in local:
        copy.start()

    barrier = pltpu.get_barrier_semaphore()
    for dx, dy in OFFSETS:
        pl.semaphore_signal(barrier, inc=1, device_id=(peer(dx, dy), d), device_id_type=MESH)

    @pl.when(first)
    def _():
        for other in range(1, DELAYS):
            pl.semaphore_signal(barrier, inc=1, device_id=(g, other), device_id_type=MESH)

    @pl.when(d == 1)
    def _():
        for other in (0, 2):
            pl.semaphore_signal(barrier, inc=1, device_id=(g, other), device_id_type=MESH)

    @pl.when(d > 1)
    def _():
        pl.semaphore_signal(barrier, inc=1, device_id=(g, 0), device_id_type=MESH)
        pl.semaphore_signal(barrier, inc=1, device_id=(g, d - 1), device_id_type=MESH)

        @pl.when(d < DELAYS - 1)
        def _():
            pl.semaphore_signal(barrier, inc=1, device_id=(g, d + 1), device_id_type=MESH)

        for j in range(1, CHIPS):
            @pl.when(j != chip)
            def _():
                pl.semaphore_signal(barrier, inc=1, device_id=(g, 2 * j + core), device_id_type=MESH)

    def enter():
        greeted = jnp.where(d == 0, 15, jnp.where(d == 1, 2, jnp.where(d == DELAYS - 1, 8, 9)))
        pl.semaphore_wait(barrier, 15 + greeted)

    def shift(n):
        return pltpu.make_async_remote_copy(
            src_ref=held.at[n], dst_ref=held.at[n + 1], send_sem=shift_send.at[n], recv_sem=shift_recv.at[n + 1],
            device_id=(g, d + 1), device_id_type=MESH,
        )

    def block_copy(n, dx, dy):
        h = peer(dx, dy)
        return pltpu.make_async_remote_copy(
            src_ref=staged.at[n, h], dst_ref=blocks.at[n, x, y],
            send_sem=block_send.at[n], recv_sem=block_recv.at[n, x],
            device_id=(h, d), device_id_type=MESH,
        )

    def all_sent(ref, sem):
        pltpu.make_async_remote_copy(
            src_ref=ref, dst_ref=ref, send_sem=sem, recv_sem=sem, device_id=(g, d + 1 - 2 * core), device_id_type=MESH,
        ).wait_send()

    def all_come(ref, sem):
        pltpu.make_async_remote_copy(
            src_ref=ref, dst_ref=ref, send_sem=sem, recv_sem=sem, device_id=(g, d + 1 - 2 * core), device_id_type=MESH,
        ).wait_recv()

    def pack(n):
        source[...] = held[n]
        for dx, dy in OFFSETS:
            h = peer(dx, dy)
            staged[n, h] = source[pick_ref[g, h]]
        blocks[n, x, y] = source[pick_ref[g, g]]

    def start_shift(n):
        @pl.when(jnp.logical_and(n < STEPS - 1, jnp.logical_and(d >= n, d < DELAYS - 1)))
        def _():
            shift(n).start()

    def send_blocks(n):
        source[...] = held[n]
        for dx, dy in OFFSETS:
            h = peer(dx, dy)
            staged[n, h] = source[pick_ref[g, h]]
            block_copy(n, dx, dy).start()
        blocks[n, x, y] = source[pick_ref[g, g]]

    def pair(n, target):
        return pltpu.make_async_remote_copy(
            src_ref=pair_out.at[n], dst_ref=pair_in.at[n], send_sem=pair_send.at[0], recv_sem=pair_recv.at[n],
            device_id=(g, target), device_id_type=MESH,
        )

    def half(n):
        return pltpu.make_async_remote_copy(
            src_ref=half_out.at[n], dst_ref=half_in.at[n], send_sem=half_send.at[0], recv_sem=half_recv.at[n],
            device_id=(g, d + 1 - 2 * core), device_id_type=MESH,
        )

    def part(n, j):
        return pltpu.make_async_remote_copy(
            src_ref=part_out.at[n, j], dst_ref=part_in.at[n, chip], send_sem=part_send.at[n],
            recv_sem=part_recv.at[n], device_id=(g, 2 * j + core), device_id_type=MESH,
        )

    def part_first(n, c, z, target):
        return pltpu.make_async_remote_copy(
            src_ref=part_out.at[n, 0], dst_ref=first_in.at[n, c, z], send_sem=part_send.at[n],
            recv_sem=first_recv.at[n], device_id=(g, target), device_id_type=MESH,
        )

    def chunk(n, c, z, target):
        return pltpu.make_async_remote_copy(
            src_ref=chunk_out.at[n], dst_ref=chunk_in.at[n, c, z], send_sem=chunk_send.at[0],
            recv_sem=chunk_recv.at[n], device_id=(g, target), device_id_type=MESH,
        )

    last = STEPS - 1

    def cast(k, j):
        rows = pl.ds(k * SLAB, SLAB)
        return pltpu.make_async_remote_copy(
            src_ref=currents.at[last, rows], dst_ref=currents.at[last, rows], send_sem=cast_send.at[last],
            recv_sem=cast_recv.at[last + k], device_id=(g, 2 * j), device_id_type=MESH,
        )

    def fan(k, target):
        rows = pl.ds(k * SLAB, SLAB)
        return pltpu.make_async_remote_copy(
            src_ref=currents.at[last, rows], dst_ref=currents.at[last, rows], send_sem=fan_send.at[last],
            recv_sem=fan_recv.at[last], device_id=(g, target), device_id_type=MESH,
        )

    def store_slab(k):
        rows = pl.ds(k * SLAB, SLAB)
        return pltpu.make_async_copy(currents.at[last, rows], out_hbm.at[last, rows], out_sem.at[0])

    def cast_all(n, j):
        return pltpu.make_async_remote_copy(
            src_ref=currents.at[n], dst_ref=currents.at[n], send_sem=cast_send.at[n],
            recv_sem=cast_recv.at[n], device_id=(g, 2 * j), device_id_type=MESH,
        )

    def fan_all(n, target):
        return pltpu.make_async_remote_copy(
            src_ref=currents.at[n], dst_ref=currents.at[n], send_sem=fan_send.at[n],
            recv_sem=fan_recv.at[n], device_id=(g, target), device_id_type=MESH,
        )

    def store(n):
        return pltpu.make_async_copy(currents.at[n], out_hbm.at[n], out_sem.at[0])

    local[0].wait()
    pack(0)
    enter()
    for dx, dy in OFFSETS:
        block_copy(0, dx, dy).start()
    start_shift(0)

    weights[GROUPS * PLACES] = jnp.zeros((BLK, BLK), weights.dtype)
    for i in range(SIDE * 2):
        rows = jnp.broadcast_to(diag_ref[i : i + 1, :], (COLS, COLS))
        rdiag[pl.ds(i * COLS, COLS), :] = 1.0 / jnp.transpose(rows)
    local[1].wait()

    def spread(hx, carry):
        for hy in range(SIDE):
            h = hx * SIDE + hy
            for r in range(SIDE):
                place = jnp.int32(GROUPS * PLACES)
                for l in range(PLACES):
                    hit = jnp.logical_and(row_ref[l, 0, h] == r, l < count_ref[h])
                    place = jnp.where(hit, h * PLACES + l, place)
                dense[hx, pl.ds(r * BLK, BLK), pl.ds(hy * BLK, BLK)] = weights[place]
        return carry

    lax.fori_loop(0, SIDE, spread, 0)
    local[2].wait()
    local[3].wait()

    def fold_sweeps():
        wide = 2 * COLS

        def scaled(t, half):
            tile = pl.ds(pl.multiple_of(t * wide + half * COLS, COLS), COLS)
            return tile, self_block[:, tile].astype(jnp.float32) * rdiag[...]

        def scale(t, carry):
            for half in range(2):
                tile, value = scaled(t, half)
                ratio[:, tile] = value.astype(jnp.bfloat16)
            return carry

        lax.fori_loop(0, ROWS // wide, scale, 0)

        def fold(factor, result):
            def body(t, carry):
                both = pl.ds(pl.multiple_of(t * wide, wide), wide)
                product = jnp.dot(ratio[...], factor[:, both], preferred_element_type=jnp.float32)
                for half in range(2):
                    tile, value = scaled(t, half)
                    part = product[:, half * COLS : half * COLS + COLS]
                    result[:, tile] = (value - part).astype(jnp.bfloat16)
                return carry

            lax.fori_loop(0, ROWS // wide, body, 0)

        fold(ratio, power)
        fold(power, self_block)

    def step(n, carry):
        def quarter(c, carry):
            hx = (x + jnp.where(c == 0, 2, jnp.where(c == 1, 3, jnp.where(c == 2, 1, 0)))) % SIDE
            @pl.when(hx == x)
            def _():
                all_come(blocks.at[n, hx, pl.ds(0, SIDE - 1)], block_recv.at[n, hx])

            @pl.when(hx != x)
            def _():
                all_come(blocks.at[n, hx], block_recv.at[n, hx])

            @pl.when(jnp.logical_and(c == 0, jnp.logical_and(first, jnp.logical_or(n == 1, n == 2))))
            def _():
                pl.semaphore_signal(turn_sem, inc=1, device_id=(g, 1), device_id_type=MESH)

            @pl.when(c == 1)
            def _():
                @pl.when(jnp.logical_and(d > n, n < STEPS - 1))
                def _():
                    shift_in = pltpu.make_async_remote_copy(
                        src_ref=held.at[n], dst_ref=held.at[n + 1], send_sem=shift_send.at[n],
                        recv_sem=shift_recv.at[n + 1], device_id=(g, d - 1), device_id_type=MESH,
                    )
                    shift_in.wait_recv()
                    start_shift(n + 1)
                    send_blocks(n + 1)

            value = jnp.dot(
                dense[hx], blocks[n, hx].reshape(ROWS, COLS), preferred_element_type=jnp.float32
            )

            @pl.when(c == 0)
            def _():
                total[...] = value

            @pl.when(c > 0)
            def _():
                total[...] += value

            return carry

        lax.fori_loop(0, SIDE, quarter, 0)

        @pl.when(d == 1)
        def _():
            pair_out[n] = total[...].astype(jnp.bfloat16)
            pair(n, 0).start()

        @pl.when(d > 1)
        def _():
            mine = pl.ds(pl.multiple_of(core * HALF, HALF), HALF)
            other = pl.ds(pl.multiple_of(HALF - core * HALF, HALF), HALF)
            half_out[n] = total[other, :].astype(jnp.bfloat16)
            half(n).start()
            half(n).wait_recv()
            summed = total[mine, :] + half_in[n].astype(jnp.float32)
            total[mine, :] = summed
            part_out[n] = summed.astype(jnp.bfloat16).reshape(CHIPS, PART, COLS)
            for j in (4, 3, 5, 2, 6, 1, 7):
                @pl.when(j != chip)
                def _():
                    part(n, j).start()
            part_first(n, core, chip, 0).start()

            @pl.when(jnp.logical_and(d == 2, n == 2))
            def _():
                cast_all(0, 0).wait_recv()
                held[n + 1] = currents[0].reshape(SIDE, BLK, COLS)
                send_blocks(n + 1)

            place = pl.ds(pl.multiple_of(core * HALF + chip * PART, PART), PART)
            all_come(part_in.at[n, pl.ds(0, CHIPS - 2)], part_recv.at[n])
            part_in[n, chip] = jnp.zeros((PART, COLS), jnp.bfloat16)
            value = total[place, :]
            for j in range(1, CHIPS):
                value += part_in[n, j].astype(jnp.float32)
            chunk_out[n] = value.astype(jnp.bfloat16)
            chunk(n, core, chip, 0).start()

        @pl.when(first)
        def _():
            pl.when(n == 0)(fold_sweeps)

            all_come(first_in.at[n, :, pl.ds(0, CHIPS - 1)], first_recv.at[n])
            all_come(chunk_in.at[n, :, pl.ds(0, CHIPS - 1)], chunk_recv.at[n])
            for c in range(2):
                value = first_in[n, c, 1].astype(jnp.float32)
                for z in range(2, CHIPS):
                    value += first_in[n, c, z].astype(jnp.float32)
                chunk_in[n, c, 0] = value.astype(jnp.bfloat16)
            pair(n, 1).wait_recv()
            value = incident[n].astype(jnp.float32) - chunk_in[n].reshape(ROWS, COLS).astype(jnp.float32)
            value = (value - pair_in[n].astype(jnp.float32) - total[...]) * rdiag[...]
            total[...] = value
            coupled = jnp.dot(self_block[...], value.astype(jnp.bfloat16), preferred_element_type=jnp.float32)
            current = (total[...] - coupled).astype(jnp.bfloat16)
            currents[n] = current

            @pl.when(n < STEPS - 1)
            def _():
                held[n + 1] = current.reshape(SIDE, BLK, COLS)
                send_blocks(n + 1)
                fan_all(n, 1).start()
                for j in (1, 4, 3, 5, 2, 6, 7):
                    cast_all(n, j).start()

            @pl.when(n == last)
            def _():
                for j in (4, 3, 5, 2, 6, 1, 7):
                    cast(j, j).start()
                for j in (4, 3, 5, 2, 6, 1, 7):
                    cast(0, j).start()
                for k in range(CHIPS):
                    fan(k, 1).start()

            store(n).start()

        @pl.when(jnp.logical_and(d == 1, jnp.logical_or(n == 1, n == 2)))
        def _():
            fan_all(n - 1, 0).wait_recv()
            held[n + 1] = currents[n - 1].reshape(SIDE, BLK, COLS)
            pack(n + 1)
            pl.semaphore_wait(turn_sem, 1)
            for dx, dy in OFFSETS:
                block_copy(n + 1, dx, dy).start()

        return carry

    lax.fori_loop(0, STEPS, step, 0)

    def finish(n, carry):
        @pl.when(jnp.logical_and(core == 0, d > 0))
        def _():
            @pl.when(jnp.logical_not(jnp.logical_and(d == 2, n == 0)))
            def _():
                cast_all(n, 0).wait_recv()

            fan_all(n, d + 1).start()
            store(n).start()

        @pl.when(core == 1)
        def _():
            @pl.when(jnp.logical_or(d > 1, n == last - 1))
            def _():
                fan_all(n, d - 1).wait_recv()

            store(n).start()

        return carry

    lax.fori_loop(0, last, finish, 0)

    @pl.when(jnp.logical_and(core == 0, d > 0))
    def _():
        cast(chip, 0).wait_recv()
        for j in (4, 3, 5, 2, 6, 1, 7):
            to = (chip + j) % CHIPS

            @pl.when(to > 0)
            def _():
                cast(chip, to).start()
        fan(chip, d + 1).start()
        store_slab(chip).start()
        for j in range(1, CHIPS):
            k = (chip + j) % CHIPS
            cast(k, 0).wait_recv()
            fan(k, d + 1).start()
            store_slab(k).start()

    @pl.when(core == 1)
    def _():
        all_come(currents.at[last], fan_recv.at[last])
        store(last).start()

    def drain(n, carry):
        all_sent(staged.at[n, pl.ds(0, GROUPS - 1)], block_send.at[n])

        @pl.when(jnp.logical_and(n < STEPS - 1, jnp.logical_and(d >= n, d < DELAYS - 1)))
        def _():
            shift(n).wait_send()

        @pl.when(d > 1)
        def _():
            all_sent(part_out.at[n, pl.ds(0, CHIPS - 1)], part_send.at[n])

        @pl.when(core == 0)
        def _():
            all_sent(currents.at[n], fan_send.at[n])

        @pl.when(jnp.logical_and(first, n < last))
        def _():
            all_sent(weights.at[pl.ds(0, 2 * CHIPS - 2)], cast_send.at[n])

        return carry

    lax.fori_loop(0, STEPS, drain, 0)

    @pl.when(d == 1)
    def _():
        all_sent(pair_out, pair_send.at[0])

    @pl.when(d > 1)
    def _():
        all_sent(half_out, half_send.at[0])
        all_sent(chunk_out, chunk_send.at[0])

    @pl.when(first)
    def _():
        all_sent(staged.at[0, pl.ds(0, CHIPS - 1)], cast_send.at[last])

    @pl.when(jnp.logical_and(core == 0, d > 0))
    def _():
        all_sent(staged.at[0, pl.ds(0, CHIPS // 2 - 1)], cast_send.at[last])

    pltpu.make_async_copy(currents, out_hbm, out_sem.at[0]).wait()


def local(retarded, block_row, block_count, send_pick, history, incident, self_block, sheet_diag):
    smem = pl.BlockSpec(memory_space=pltpu.SMEM)
    vmem = pl.BlockSpec(memory_space=pltpu.VMEM)
    hbm = pl.BlockSpec(memory_space=pl.ANY)
    bf16, f32 = jnp.bfloat16, jnp.float32
    dma = pltpu.SemaphoreType.DMA
    call = pl.pallas_call(
        kernel,
        out_shape=jax.ShapeDtypeStruct((STEPS, ROWS, COLS), bf16),
        in_specs=[smem, smem, smem, hbm, hbm, hbm, hbm, vmem],
        out_specs=hbm,
        scratch_shapes=[
            pltpu.VMEM((GROUPS * PLACES + 1, BLK, BLK), bf16),
            pltpu.VMEM((SIDE, ROWS, ROWS), bf16),
            pltpu.VMEM((ROWS, ROWS), bf16),
            pltpu.VMEM((ROWS, ROWS), bf16),
            pltpu.VMEM((ROWS, ROWS), bf16),
            pltpu.VMEM((STEPS, ROWS, COLS), bf16),
            pltpu.VMEM((STEPS, SIDE, BLK, COLS), bf16),
            pltpu.VMEM((SIDE, BLK, COLS), bf16),
            pltpu.VMEM((STEPS, GROUPS, BLK, COLS), bf16),
            pltpu.VMEM((STEPS, SIDE, SIDE, BLK, COLS), bf16),
            pltpu.VMEM((ROWS, COLS), f32),
            pltpu.VMEM((ROWS, COLS), f32),
            pltpu.VMEM((STEPS, ROWS, COLS), bf16),
            pltpu.VMEM((STEPS, ROWS, COLS), bf16),
            pltpu.VMEM((STEPS, HALF, COLS), bf16),
            pltpu.VMEM((STEPS, HALF, COLS), bf16),
            pltpu.VMEM((STEPS, CHIPS, PART, COLS), bf16),
            pltpu.VMEM((STEPS, CHIPS, PART, COLS), bf16),
            pltpu.VMEM((STEPS, PART, COLS), bf16),
            pltpu.VMEM((STEPS, 2, CHIPS, PART, COLS), bf16),
            pltpu.VMEM((STEPS, 2, CHIPS, PART, COLS), bf16),
            pltpu.VMEM((STEPS, ROWS, COLS), bf16),
            dma((4,)),
            dma((STEPS,)), dma((STEPS, SIDE)),
            dma((STEPS,)), dma((STEPS,)),
            dma((1,)), dma((STEPS,)),
            dma((1,)), dma((STEPS,)),
            dma((STEPS,)), dma((STEPS,)),
            dma((1,)), dma((STEPS,)), dma((STEPS,)),
            dma((STEPS,)), dma((STEPS + CHIPS,)),
            dma((STEPS,)), dma((STEPS,)),
            dma((1,)),
            pltpu.SemaphoreType.REGULAR,
        ],
        compiler_params=pltpu.CompilerParams(
            collective_id=0, has_side_effects=True, vmem_limit_bytes=56 * 2**20
        ),
        cost_estimate=pl.CostEstimate(flops=8 * 10**9, bytes_accessed=12 * 10**6, transcendentals=0),
    )
    return call(
        jnp.transpose(block_row, (2, 0, 1)), block_count[0], send_pick[0],
        retarded.reshape(GROUPS * PLACES, BLK, BLK), history.reshape(SIDE, BLK, COLS),
        incident, self_block, sheet_diag.reshape(SIDE * 2, COLS),
    )


def solution(mesh):
    placed = (
        P("delay", "group", None, None, None),
        P("delay", "group", None),
        P("delay", "group"),
        P("delay", None, None),
        P("delay", "group", None),
        P(None, "group", None),
        P("group", None),
        P("group"),
    )
    return jax.shard_map(
        local, mesh=mesh, in_specs=placed, out_specs=P(None, "group", None), check_vma=False
    )
```
